32 devices in a mesh: grp: 2 (over x), row: 16 (over z, y, core).
Axes of the slice: x: 2, y: 2, z: 4, core: 2. Of those that a mesh axis runs over, the one named last changes fastest.
Arguments:
- s1_embed: bfloat16 [16384, 768], P(('grp', 'row')), parts along dimension 0, may hold values from -40 to 40
- s2_embed: bfloat16 [16384, 768], P(('grp', 'row')), parts along dimension 0, may hold values from -40 to 40
- block_list: int32 [128, 4], P('grp'), parts along dimension 0, may hold values from 0 to 63, as said below
- footprint: int32 [16384], P('grp'), parts along dimension 0, may hold values from 0 to 2729, never falling along the last dimension, each value on 1 to 4 neighbouring positions
Outputs:
- grad_s1: float32 [16384, 768], P(('grp', 'row')), parts along dimension 0
- grad_s2: float32 [16384, 768], P(('grp', 'row')), parts along dimension 0
The draws below stay inside these ranges and needn't reach their ends.
There are 2 independent parts, one for each index of `grp`. The reference program is written for one: setup_inputs(seed, part) draws one part's arguments, and reference() takes and returns one part's arrays. A program takes and returns all parts, laid end to end along the dimension named above; each array names one. Nothing has to cross between parts.
Inputs may be any that keep to these rules, and one draw needn't show every extreme that they name: Row r of block_list holds 4 distinct column blocks, the first being r itself; for every listed column block c, c // 4 differs from r // 4 by at most 3, counted cyclically over the devices of the row axis.
All inputs are finite; a program needn't handle non-finite values.
Results may differ from the reference program's by a relative error of at most 0.0016.
Values may be sent and summed in bfloat16 or wider, within the bound.
A program may use at most 128 MiB of HBM per device.

```python
import math
import jax
import jax.numpy as jnp
import numpy as np
from jax import lax

D = 768
BLK = 128
HALF = 3
RB = 4
NPAIR = 8192
NRB = 64
KB = 4


def base_embed(key):
    return jnp.clip(jax.random.normal(jax.random.fold_in(key, 1), (NPAIR, D), jnp.float32), -6.0, 6.0) * 0.35


def draw_s1_embed(key, part):
    values = base_embed(jax.random.fold_in(key, 21))
    return values.astype(jnp.bfloat16)


def draw_s2_embed(key, part):
    values = base_embed(jax.random.fold_in(key, 22))
    return values.astype(jnp.bfloat16)


def draw_block_list(key, part):
    devices = NRB // RB
    span = 2 * HALF + 1
    rows = jnp.arange(NRB, dtype=jnp.int32)
    owner = rows // RB
    slots = jnp.arange(span * RB, dtype=jnp.int32)
    candidate = (owner[:, None] + slots[None, :] // RB - HALF + devices) % devices * RB + slots[None, :] % RB
    popular = (jax.random.randint(jax.random.fold_in(key, 3), (devices,), 0, 4) == 0).astype(jnp.int32)
    score = jax.random.randint(jax.random.fold_in(key, 4), (NRB, span * RB), 0, 1024) + 1024 * popular[candidate // RB]
    score = score * 4096 + slots[None, :]
    score = jnp.where(candidate == rows[:, None], -1, score)
    unused, picked = lax.top_k(score, KB - 1)
    listed = jnp.take_along_axis(candidate, picked, axis=1)
    return jnp.concatenate([rows[:, None], listed], axis=1).astype(jnp.int32)


def split_up(amount, total, most, slope):
    weights = [(1 << 20) // math.isqrt(standing ** slope) + 1 for standing in range(2, amount + 1)]
    surplus, holding = total - most - (amount - 1), [1] * (amount - 1)
    while surplus > 0:
        candidates = [i for i in range(amount - 1) if holding[i] < most]
        whole, budget = sum([weights[i] for i in candidates]), surplus
        for i in candidates:
            more = min(most - holding[i], max(1, budget * weights[i] // whole), surplus)
            holding[i] = holding[i] + more
            surplus = surplus - more
    return np.array([most] + holding)


def uneven(own_key, count, total, reach, lean):
    if count == 2:
        one = jax.random.randint(own_key, (), max(1, total - reach), min(reach, total - 1) + 1)
        return jnp.stack([one, total - one])
    tallies = jnp.asarray(split_up(count, total, reach, lean), jnp.int32)
    twos = (count - 1) // 2
    source_of, receiver = tallies[1:1 + 2 * twos:2], tallies[2:2 + 2 * twos:2]
    margin = jnp.minimum(source_of - 1, reach - receiver)
    shifted = jax.random.randint(jax.random.fold_in(own_key, 1), (twos,), 0, 1 << 20) % (margin + 1)
    tallies = tallies.at[1:1 + 2 * twos:2].set(source_of - shifted).at[2:2 + 2 * twos:2].set(receiver + shifted)
    return tallies[jax.random.permutation(jax.random.fold_in(own_key, 2), count)]


def setup_inputs(seed: int = 0, part: int = 0) -> dict:
    keys = jax.random.split(jax.random.key(seed), 5)
    own_keys = jax.random.split(jax.random.fold_in(keys[4], part), 5)
    return {
        "s1_embed": draw_s1_embed(jax.random.fold_in(jax.random.fold_in(keys[4], part), 71), part),
        "s2_embed": draw_s2_embed(jax.random.fold_in(jax.random.fold_in(keys[4], part), 71), part),
        "block_list": draw_block_list(jax.random.fold_in(jax.random.fold_in(keys[4], part), 71), part),
        "footprint": jnp.searchsorted(jnp.cumsum(uneven(own_keys[3], NPAIR // 3, NPAIR, 4, 0)), jnp.arange(NPAIR), side="right").astype(jnp.int32),
    }


NEGATIVE = -1e30


def block_scores(s1_embed, s2_embed, block_list, footprint, block):
    within = jnp.arange(BLK, dtype=jnp.int32)
    column_ids = (block_list[block][:, None] * BLK + within[None, :]).reshape(-1).astype(jnp.int32)
    row_ids = (block * BLK + within).astype(jnp.int32)
    row_part = lax.dynamic_slice_in_dim(s1_embed, block * BLK, BLK, 0)
    column_part = jnp.take(s2_embed, column_ids, axis=0)
    scores = jnp.dot(row_part, column_part.T, preferred_element_type=jnp.float32)
    foot_rows = lax.dynamic_slice_in_dim(footprint, block * BLK, BLK, 0)
    foot_columns = jnp.take(footprint, column_ids, axis=0)
    diagonal = row_ids[:, None] == column_ids[None, :]
    valid = (foot_rows[:, None] != foot_columns[None, :]) | diagonal
    masked = jnp.where(valid, scores, NEGATIVE)
    return masked, valid, diagonal, column_ids, row_part, column_part


def reference(s1_embed, s2_embed, block_list, footprint):
    blocks = jnp.arange(NRB, dtype=jnp.int32)

    def forward(carry, block):
        column_top, column_total = carry
        masked, valid, diagonal, column_ids, row_part, column_part = block_scores(s1_embed, s2_embed, block_list, footprint, block)
        row_top = jnp.max(masked, axis=1)
        row_total = jnp.sum(jnp.where(valid, jnp.exp(masked - row_top[:, None]), 0.0), axis=1)
        part_top = jnp.max(masked, axis=0)
        part_total = jnp.sum(jnp.where(valid, jnp.exp(masked - part_top[None, :]), 0.0), axis=0)
        old_top = column_top[column_ids]
        old_total = column_total[column_ids]
        new_top = jnp.maximum(old_top, part_top)
        new_total = old_total * jnp.exp(old_top - new_top) + part_total * jnp.exp(part_top - new_top)
        column_top = column_top.at[column_ids].set(new_top)
        column_total = column_total.at[column_ids].set(new_total)
        return (column_top, column_total), row_top + jnp.log(row_total)

    start = (jnp.full((NPAIR,), NEGATIVE, jnp.float32), jnp.zeros((NPAIR,), jnp.float32))
    (column_top, column_total), row_level = lax.scan(forward, start, blocks)
    row_level = row_level.reshape(NPAIR)
    column_level = column_top + jnp.log(column_total)

    def backward(grad_s2, block):
        masked, valid, diagonal, column_ids, row_part, column_part = block_scores(s1_embed, s2_embed, block_list, footprint, block)
        level_rows = lax.dynamic_slice_in_dim(row_level, block * BLK, BLK, 0)
        p_row = jnp.where(valid, jnp.exp(masked - level_rows[:, None]), 0.0)
        p_column = jnp.where(valid, jnp.exp(masked - column_level[column_ids][None, :]), 0.0)
        weights = (0.5 * (p_row + p_column) - jnp.where(diagonal, 1.0, 0.0)).astype(jnp.bfloat16)
        to_rows = jnp.dot(weights, column_part, preferred_element_type=jnp.float32)
        to_columns = jnp.dot(weights.T, row_part, preferred_element_type=jnp.float32)
        grad_s2 = grad_s2.at[column_ids].add(to_columns)
        return grad_s2, to_rows

    grad_s2, grad_rows = lax.scan(backward, jnp.zeros((NPAIR, D), jnp.float32), blocks)
    return grad_rows.reshape(NPAIR, D), grad_s2
```

```python
import functools

import jax
import jax.numpy as jnp
from jax import lax
from jax.experimental import pallas as pl
from jax.experimental.pallas import tpu as pltpu
from jax.sharding import PartitionSpec as P

BLK = 128
NEGATIVE = -1e30
ROLES = 6
OWN = 6
MESH = pl.DeviceIdType.MESH


def kernel(
    n, s1, s2, blist, foot, g1, g2,
    win, logit, act, footw, footc, mx, sm, levc, levw,
    send_sem, recv_sem, lev_send, lev_recv,
):
    rows, width = s1.shape
    nb = rows // BLK
    kb = blist.shape[1]
    tile = min(256, rows)
    me = lax.axis_index("row")
    sgn = 1 - 2 * lax.rem(me, 2)

    def dev(offset):
        return lax.rem(me + offset + n, n)

    source = [dev(sgn), dev(-2), dev(2), dev(-3 * sgn), dev(sgn - 2), dev(sgn + 2)]
    target = [dev(sgn), dev(2), dev(-2), dev(-3 * sgn), dev(sgn + 2), dev(sgn - 2)]

    barrier = pltpu.get_barrier_semaphore()
    for r in range(ROLES):
        pl.semaphore_signal(barrier, inc=1, device_id={"row": target[r]}, device_id_type=MESH)
    pl.semaphore_wait(barrier, ROLES)

    own_left = (s1, s2)
    own_right = (s2, s1)

    def direct(kind, role):
        return pltpu.make_async_remote_copy(
            src_ref=own_right[kind], dst_ref=win.at[kind, role],
            send_sem=send_sem.at[kind, role], recv_sem=recv_sem.at[kind, role],
            device_id={"row": target[role]}, device_id_type=MESH,
        )

    def forward(kind, role):
        return pltpu.make_async_remote_copy(
            src_ref=win.at[kind, role - 3], dst_ref=win.at[kind, role],
            send_sem=send_sem.at[kind, role], recv_sem=recv_sem.at[kind, role],
            device_id={"row": target[0]}, device_id_type=MESH,
        )

    def level_copy(kind, role):
        return pltpu.make_async_remote_copy(
            src_ref=levw.at[kind, OWN], dst_ref=levw.at[kind, role],
            send_sem=lev_send.at[kind, role], recv_sem=lev_recv.at[kind, role],
            device_id={"row": target[role]}, device_id_type=MESH,
        )

    for kind in range(2):
        for role in (3, 1, 2, 0):
            direct(kind, role).start()

    lane_block = lax.broadcasted_iota(jnp.int32, (1, rows), 1) // BLK
    for slot, owner in enumerate(source + [me]):
        footw[slot, 0:1, :] = foot[pl.ds(owner, 1), :]
        columns = lane_block + owner * nb
        for b in range(nb):
            hit = jnp.zeros((1, rows), jnp.float32)
            for k in range(kb):
                hit = jnp.where(columns == blist[me * nb + b, k], 1.0, hit)
            act[0, slot, b : b + 1, :] = hit
        hits = [jnp.zeros((1, rows), jnp.float32) for _ in range(nb)]
        for k in range(kb):
            listed = jnp.full((1, rows), blist[owner * nb, k], jnp.int32)
            for b in range(1, nb):
                listed = jnp.where(lane_block == b, blist[owner * nb + b, k], listed)
            for b in range(nb):
                hits[b] = jnp.where(listed == me * nb + b, 1.0, hits[b])
        for b in range(nb):
            act[1, slot, b : b + 1, :] = hits[b]
    footc[...] = jnp.transpose(jnp.broadcast_to(foot[pl.ds(me, 1), :], (BLK, rows)))
    mx[...] = jnp.full(mx.shape, NEGATIVE, jnp.float32)
    sm[...] = jnp.zeros(sm.shape, jnp.float32)
    eye = lax.broadcasted_iota(jnp.int32, (BLK, BLK), 0) == lax.broadcasted_iota(
        jnp.int32, (BLK, BLK), 1
    )

    def stats(kind, slot, right, diag):
        for t in range(rows // tile):
            raw = lax.dot_general(
                own_left[kind][t * tile : (t + 1) * tile, :], right,
                (((1,), (1,)), ((), ())), preferred_element_type=jnp.float32,
            )
            for u in range(tile // BLK):
                b = t * (tile // BLK) + u
                span = slice(b * BLK, (b + 1) * BLK)
                top = mx[kind, span, :]
                new = top
                parts = []
                for j in range(nb):
                    cols = slice(j * BLK, (j + 1) * BLK)
                    valid = footc[span, :] != footw[slot, 0:1, cols]
                    if diag and j == b:
                        valid = jnp.logical_or(valid, eye)
                    valid = jnp.logical_and(valid, act[kind, slot, b : b + 1, cols] > 0.0)
                    part = jnp.where(valid, raw[u * BLK : (u + 1) * BLK, cols], NEGATIVE)
                    logit[kind, slot, span, cols] = part
                    parts.append(part)
                    new = jnp.maximum(new, part)
                total = sm[kind, span, :] * jnp.exp(top - new)
                for part in parts:
                    total = total + jnp.exp(part - new)
                mx[kind, span, :] = new
                sm[kind, span, :] = total

    def levels(kind):
        top = mx[kind]
        highest = jnp.max(top, axis=1, keepdims=True)
        total = jnp.sum(sm[kind] * jnp.exp(top - highest), axis=1, keepdims=True)
        wide = jnp.broadcast_to(highest + jnp.log(total), (rows, BLK))
        levc[kind] = wide
        levw[kind, OWN] = jnp.transpose(wide)[0:8, :]
        for role in range(ROLES):
            level_copy(kind, role).start()

    for kind in range(2):
        stats(kind, OWN, own_right[kind][...], True)

    for kind in range(2):

        def arrive(role, carry, kind=kind):
            pltpu.make_async_copy(win.at[kind, role], win.at[kind, role], recv_sem.at[kind, role]).wait()

            @pl.when(jnp.logical_or(role == 1, role == 2))
            def _():
                pltpu.make_async_remote_copy(
                    src_ref=win.at[kind, role], dst_ref=win.at[kind, role + 3],
                    send_sem=send_sem.at[kind, role + 3], recv_sem=recv_sem.at[kind, role + 3],
                    device_id={"row": target[0]}, device_id_type=MESH,
                ).start()

            stats(kind, role, win[kind, role], False)
            return carry

        lax.fori_loop(0, ROLES, arrive, 0)
        levels(kind)

    def grads(kind, slot, right, out, diag):
        for t in range(rows // tile):
            pieces = []
            for u in range(tile // BLK):
                b = t * (tile // BLK) + u
                span = slice(b * BLK, (b + 1) * BLK)
                mine = levc[kind, span, :]
                across = []
                for j in range(nb):
                    cols = slice(j * BLK, (j + 1) * BLK)
                    part = logit[kind, slot, span, cols]
                    weight = 0.5 * (
                        jnp.exp(part - mine) + jnp.exp(part - levw[1 - kind, slot, 0:1, cols])
                    )
                    if diag and j == b:
                        weight = weight - jnp.where(eye, 1.0, 0.0)
                    across.append(weight.astype(jnp.bfloat16))
                pieces.append(jnp.concatenate(across, axis=1))
            weights = jnp.concatenate(pieces, axis=0)
            part = jnp.dot(weights, right, preferred_element_type=jnp.float32)
            span = slice(t * tile, (t + 1) * tile)
            if diag:
                out[span, :] = part
            else:
                out[span, :] = out[span, :] + part

    outs = (g1, g2)
    for kind in (1, 0):
        grads(kind, OWN, own_right[kind][...], outs[kind], True)

        def step(role, carry, kind=kind):
            other = levw.at[1 - kind, role]
            pltpu.make_async_copy(other, other, lev_recv.at[1 - kind, role]).wait()
            grads(kind, role, win[kind, role], outs[kind], False)
            return carry

        lax.fori_loop(0, ROLES, step, 0)

    for kind in range(2):
        for role in range(4):
            direct(kind, role).wait_send()
        for role in range(4, 6):
            forward(kind, role).wait_send()
        for role in range(ROLES):
            level_copy(kind, role).wait_send()


def shards(s1_embed, s2_embed, block_list, footprint):
    rows, width = s1_embed.shape
    n = lax.axis_size("row")
    foot = footprint.astype(jnp.float32).reshape(n, rows)
    vmem = pl.BlockSpec(memory_space=pltpu.VMEM)
    return pl.pallas_call(
        functools.partial(kernel, n),
        out_shape=(
            jax.ShapeDtypeStruct((rows, width), jnp.float32),
            jax.ShapeDtypeStruct((rows, width), jnp.float32),
        ),
        in_specs=[vmem, vmem, pl.BlockSpec(memory_space=pltpu.SMEM), vmem],
        out_specs=(vmem, vmem),
        scratch_shapes=[
            pltpu.VMEM((2, ROLES, rows, width), jnp.bfloat16),
            pltpu.VMEM((2, ROLES + 1, rows, rows), jnp.float32),
            pltpu.VMEM((2, ROLES + 1, 8, rows), jnp.float32),
            pltpu.VMEM((ROLES + 1, 8, rows), jnp.float32),
            pltpu.VMEM((rows, BLK), jnp.float32),
            pltpu.VMEM((2, rows, BLK), jnp.float32),
            pltpu.VMEM((2, rows, BLK), jnp.float32),
            pltpu.VMEM((2, rows, BLK), jnp.float32),
            pltpu.VMEM((2, ROLES + 1, 8, rows), jnp.float32),
            pltpu.SemaphoreType.DMA((2, ROLES)),
            pltpu.SemaphoreType.DMA((2, ROLES)),
            pltpu.SemaphoreType.DMA((2, ROLES)),
            pltpu.SemaphoreType.DMA((2, ROLES)),
        ],
        compiler_params=pltpu.CompilerParams(
            collective_id=0, has_side_effects=True, vmem_limit_bytes=52 * 1024 * 1024
        ),
    )(s1_embed, s2_embed, block_list, foot)


def solution(mesh):
    placed = (P(("grp", "row"), None), P(("grp", "row"), None), P("grp", None), P("grp"))
    return jax.shard_map(
        shards,
        mesh=mesh,
        in_specs=placed,
        out_specs=(P(("grp", "row"), None), P(("grp", "row"), None)),
        check_vma=False,
    )
```

```python
import functools

import jax
import jax.numpy as jnp
from jax import lax
from jax.experimental import pallas as pl
from jax.experimental.pallas import tpu as pltpu
from jax.sharding import PartitionSpec as P

BLK = 128
NEGATIVE = -1e30
ROLES = 6
OWN = 6
MESH = pl.DeviceIdType.MESH


def kernel(
    n, s1, s2, blist, foot, g1, g2,
    win, logit, act, footw, footc, mx, sm, levc, levw,
    send_sem, recv_sem, lev_send, lev_recv,
):
    rows, width = s1.shape
    nb = rows // BLK
    kb = blist.shape[1]
    tile = min(256, rows)
    me = lax.axis_index("row")
    core = lax.rem(me, 2)
    chip = me // 2
    side = lax.rem(chip, 2)
    sgn = 1 - 2 * core
    sy = 1 - 2 * side
    odd = lax.rem(core + side, 2)

    def dev(offset):
        return lax.rem(me + offset + n, n)

    def at_chip(offset, which):
        return lax.rem(2 * (chip + offset) + which + n, n)

    partner, across, straight = dev(sgn), dev(2 * sy), dev(-3 * sgn)
    source = [
        partner, across, straight, dev(2 * sy + sgn), at_chip(-sy, 1 - side), at_chip(-sy, side)
    ]
    target = [partner, across, straight, dev(2 * sy + sgn), at_chip(-sy, 0), at_chip(-sy, 1)]
    landing = [0, 1, 2, 3, 4 + odd, 4 + odd]
    relay_to = dev(sy * (5 - 3 * odd))
    relay_peer = dev(sy * (5 - 10 * odd))

    barrier = pltpu.get_barrier_semaphore()
    for peer in target + [relay_peer]:
        pl.semaphore_signal(barrier, inc=1, device_id={"row": peer}, device_id_type=MESH)
    pl.semaphore_wait(barrier, ROLES + 1)

    own_left = (s1, s2)
    own_right = (s2, s1)

    def direct(kind, role):
        return pltpu.make_async_remote_copy(
            src_ref=own_right[kind], dst_ref=win.at[kind, role],
            send_sem=send_sem.at[kind, role], recv_sem=recv_sem.at[kind, role],
            device_id={"row": target[role]}, device_id_type=MESH,
        )

    def passed(kind, held, slot, sem, to):
        return pltpu.make_async_remote_copy(
            src_ref=win.at[kind, held], dst_ref=win.at[kind, slot],
            send_sem=send_sem.at[kind, sem], recv_sem=recv_sem.at[kind, slot],
            device_id={"row": to}, device_id_type=MESH,
        )

    def hand_over(kind):
        return passed(kind, 1, 3, 3, partner)

    def relay(kind):
        return passed(kind, 1 + odd, 5 - odd, 4, relay_to)

    def share(kind):
        return passed(kind, 4 + odd, 4 + odd, 5, partner)

    def level_copy(kind, role):
        return pltpu.make_async_remote_copy(
            src_ref=levw.at[kind, OWN], dst_ref=levw.at[kind, landing[role]],
            send_sem=lev_send.at[kind, role], recv_sem=lev_recv.at[kind, landing[role]],
            device_id={"row": target[role]}, device_id_type=MESH,
        )

    for kind in range(2):
        for role in (2, 1, 0):
            direct(kind, role).start()

    lane_block = lax.broadcasted_iota(jnp.int32, (1, rows), 1) // BLK
    for slot, owner in enumerate(source + [me]):
        footw[slot, 0:1, :] = foot[pl.ds(owner, 1), :]
        columns = lane_block + owner * nb
        for b in range(nb):
            hit = jnp.zeros((1, rows), jnp.float32)
            for k in range(kb):
                hit = jnp.where(columns == blist[me * nb + b, k], 1.0, hit)
            act[0, slot, b : b + 1, :] = hit
        hits = [jnp.zeros((1, rows), jnp.float32) for _ in range(nb)]
        for k in range(kb):
            listed = jnp.full((1, rows), blist[owner * nb, k], jnp.int32)
            for b in range(1, nb):
                listed = jnp.where(lane_block == b, blist[owner * nb + b, k], listed)
            for b in range(nb):
                hits[b] = jnp.where(listed == me * nb + b, 1.0, hits[b])
        for b in range(nb):
            act[1, slot, b : b + 1, :] = hits[b]
    footc[...] = jnp.transpose(jnp.broadcast_to(foot[pl.ds(me, 1), :], (BLK, rows)))
    mx[...] = jnp.full(mx.shape, NEGATIVE, jnp.float32)
    sm[...] = jnp.zeros(sm.shape, jnp.float32)
    eye = lax.broadcasted_iota(jnp.int32, (BLK, BLK), 0) == lax.broadcasted_iota(
        jnp.int32, (BLK, BLK), 1
    )

    def stats(kind, slot, right, diag):
        for t in range(rows // tile):
            raw = lax.dot_general(
                own_left[kind][t * tile : (t + 1) * tile, :], right,
                (((1,), (1,)), ((), ())), preferred_element_type=jnp.float32,
            )
            for u in range(tile // BLK):
                b = t * (tile // BLK) + u
                span = slice(b * BLK, (b + 1) * BLK)
                top = mx[kind, span, :]
                new = top
                parts = []
                for j in range(nb):
                    cols = slice(j * BLK, (j + 1) * BLK)
                    valid = footc[span, :] != footw[slot, 0:1, cols]
                    if diag and j == b:
                        valid = jnp.logical_or(valid, eye)
                    valid = jnp.logical_and(valid, act[kind, slot, b : b + 1, cols] > 0.0)
                    part = jnp.where(valid, raw[u * BLK : (u + 1) * BLK, cols], NEGATIVE)
                    logit[kind, slot, span, cols] = part
                    parts.append(part)
                    new = jnp.maximum(new, part)
                total = sm[kind, span, :] * jnp.exp(top - new)
                for part in parts:
                    total = total + jnp.exp(part - new)
                mx[kind, span, :] = new
                sm[kind, span, :] = total

    def levels(kind):
        top = mx[kind]
        highest = jnp.max(top, axis=1, keepdims=True)
        total = jnp.sum(sm[kind] * jnp.exp(top - highest), axis=1, keepdims=True)
        wide = jnp.broadcast_to(highest + jnp.log(total), (rows, BLK))
        levc[kind] = wide
        levw[kind, OWN] = jnp.transpose(wide)[0:8, :]
        for role in range(ROLES):
            level_copy(kind, role).start()

    for kind in range(2):
        stats(kind, OWN, own_right[kind][...], True)

    def landed(kind, slot):
        block = win.at[kind, slot]
        pltpu.make_async_copy(block, block, recv_sem.at[kind, slot]).wait()

    for kind in range(2):

        def near(slot, carry, kind=kind):
            landed(kind, slot)

            @pl.when(slot == 1)
            def _():
                hand_over(kind).start()

            @pl.when(slot == 1 + odd)
            def _():
                relay(kind).start()

            stats(kind, slot, win[kind, slot], False)
            return carry

        lax.fori_loop(0, 4, near, 0)

    for kind in range(2):

        def far(j, carry, kind=kind):
            slot = 4 + lax.rem(odd + j, 2)
            landed(kind, slot)

            @pl.when(j == 0)
            def _():
                share(kind).start()

            stats(kind, slot, win[kind, slot], False)
            return carry

        lax.fori_loop(0, 2, far, 0)
        levels(kind)

    def grads(kind, slot, right, out, diag):
        for t in range(rows // tile):
            pieces = []
            for u in range(tile // BLK):
                b = t * (tile // BLK) + u
                span = slice(b * BLK, (b + 1) * BLK)
                mine = levc[kind, span, :]
                across = []
                for j in range(nb):
                    cols = slice(j * BLK, (j + 1) * BLK)
                    part = logit[kind, slot, span, cols]
                    weight = 0.5 * (
                        jnp.exp(part - mine) + jnp.exp(part - levw[1 - kind, slot, 0:1, cols])
                    )
                    if diag and j == b:
                        weight = weight - jnp.where(eye, 1.0, 0.0)
                    across.append(weight.astype(jnp.bfloat16))
                pieces.append(jnp.concatenate(across, axis=1))
            weights = jnp.concatenate(pieces, axis=0)
            part = jnp.dot(weights, right, preferred_element_type=jnp.float32)
            span = slice(t * tile, (t + 1) * tile)
            if diag:
                out[span, :] = part
            else:
                out[span, :] = out[span, :] + part

    outs = (g1, g2)
    for kind in (1, 0):
        grads(kind, OWN, own_right[kind][...], outs[kind], True)

        def step(role, carry, kind=kind):
            other = levw.at[1 - kind, role]
            pltpu.make_async_copy(other, other, lev_recv.at[1 - kind, role]).wait()
            grads(kind, role, win[kind, role], outs[kind], False)
            return carry

        lax.fori_loop(0, ROLES, step, 0)

    for kind in range(2):
        for role in range(3):
            direct(kind, role).wait_send()
        hand_over(kind).wait_send()
        relay(kind).wait_send()
        share(kind).wait_send()
        for role in range(ROLES):
            level_copy(kind, role).wait_send()


def shards(s1_embed, s2_embed, block_list, footprint):
    rows, width = s1_embed.shape
    n = lax.axis_size("row")
    foot = footprint.astype(jnp.float32).reshape(n, rows)
    vmem = pl.BlockSpec(memory_space=pltpu.VMEM)
    return pl.pallas_call(
        functools.partial(kernel, n),
        out_shape=(
            jax.ShapeDtypeStruct((rows, width), jnp.float32),
            jax.ShapeDtypeStruct((rows, width), jnp.float32),
        ),
        in_specs=[vmem, vmem, pl.BlockSpec(memory_space=pltpu.SMEM), vmem],
        out_specs=(vmem, vmem),
        scratch_shapes=[
            pltpu.VMEM((2, ROLES, rows, width), jnp.bfloat16),
            pltpu.VMEM((2, ROLES + 1, rows, rows), jnp.float32),
            pltpu.VMEM((2, ROLES + 1, 8, rows), jnp.float32),
            pltpu.VMEM((ROLES + 1, 8, rows), jnp.float32),
            pltpu.VMEM((rows, BLK), jnp.float32),
            pltpu.VMEM((2, rows, BLK), jnp.float32),
            pltpu.VMEM((2, rows, BLK), jnp.float32),
            pltpu.VMEM((2, rows, BLK), jnp.float32),
            pltpu.VMEM((2, ROLES + 1, 8, rows), jnp.float32),
            pltpu.SemaphoreType.DMA((2, ROLES)),
            pltpu.SemaphoreType.DMA((2, ROLES)),
            pltpu.SemaphoreType.DMA((2, ROLES)),
            pltpu.SemaphoreType.DMA((2, ROLES)),
        ],
        compiler_params=pltpu.CompilerParams(
            collective_id=0, has_side_effects=True, vmem_limit_bytes=52 * 1024 * 1024
        ),
    )(s1_embed, s2_embed, block_list, foot)


def solution(mesh):
    placed = (P(("grp", "row"), None), P(("grp", "row"), None), P("grp", None), P("grp"))
    return jax.shard_map(
        shards,
        mesh=mesh,
        in_specs=placed,
        out_specs=(P(("grp", "row"), None), P(("grp", "row"), None)),
        check_vma=False,
    )
```

```python
import functools

import jax
import jax.numpy as jnp
from jax import lax
from jax.experimental import pallas as pl
from jax.experimental.pallas import tpu as pltpu
from jax.sharding import PartitionSpec as P

BLK = 128
NEGATIVE = -1e30
ROLES = 6
OWN = 6
MESH = pl.DeviceIdType.MESH


def kernel(
    n, s1, s2, blist, foot_all, g1, g2,
    own, foot, load_sem, win, logit, act, footw, footc, mx, sm, levc, levw,
    send_sem, recv_sem, lev_send, lev_recv,
):
    rows, width = s1.shape
    nb = rows // BLK
    kb = blist.shape[0]
    tile = min(256, rows)
    me = lax.axis_index("row")
    core = lax.rem(me, 2)
    chip = me // 2
    side = lax.rem(chip, 2)
    sgn = 1 - 2 * core
    sy = 1 - 2 * side
    odd = lax.rem(core + side, 2)

    def dev(offset):
        return lax.rem(me + offset + n, n)

    def at_chip(offset, which):
        return lax.rem(2 * (chip + offset) + which + n, n)

    partner, across, straight = dev(sgn), dev(2 * sy), dev(-3 * sgn)
    source = [
        partner, across, straight, dev(2 * sy + sgn), at_chip(-sy, 1 - side), at_chip(-sy, side)
    ]
    target = [partner, across, straight, dev(2 * sy + sgn), at_chip(-sy, 0), at_chip(-sy, 1)]
    landing = [0, 1, 2, 3, 4 + odd, 4 + odd]
    relay_to = dev(sy * (5 - 3 * odd))
    relay_peer = dev(sy * (5 - 10 * odd))

    barrier = pltpu.get_barrier_semaphore()
    for peer in target + [relay_peer]:
        pl.semaphore_signal(barrier, inc=1, device_id={"row": peer}, device_id_type=MESH)
    pl.semaphore_wait(barrier, ROLES + 1)

    own_right = (s2, s1)

    def direct(kind, role):
        return pltpu.make_async_remote_copy(
            src_ref=own_right[kind], dst_ref=win.at[kind, role],
            send_sem=send_sem.at[kind, role], recv_sem=recv_sem.at[kind, role],
            device_id={"row": target[role]}, device_id_type=MESH,
        )

    def passed(kind, held, slot, sem, to):
        return pltpu.make_async_remote_copy(
            src_ref=win.at[kind, held], dst_ref=win.at[kind, slot],
            send_sem=send_sem.at[kind, sem], recv_sem=recv_sem.at[kind, slot],
            device_id={"row": to}, device_id_type=MESH,
        )

    def hand_over(kind):
        return passed(kind, 1, 3, 3, partner)

    def relay(kind):
        return passed(kind, 1 + odd, 5 - odd, 4, relay_to)

    def share(kind):
        return passed(kind, 4 + odd, 4 + odd, 5, partner)

    def level_copy(kind, role):
        return pltpu.make_async_remote_copy(
            src_ref=levw.at[kind, OWN], dst_ref=levw.at[kind, landing[role]],
            send_sem=lev_send.at[kind, role], recv_sem=lev_recv.at[kind, landing[role]],
            device_id={"row": target[role]}, device_id_type=MESH,
        )

    for kind in range(2):
        for role in (2, 1, 0):
            direct(kind, role).start()

    loads = [
        pltpu.make_async_copy(foot_all, foot, load_sem.at[2]),
        pltpu.make_async_copy(s1, own.at[0], load_sem.at[0]),
        pltpu.make_async_copy(s2, own.at[1], load_sem.at[1]),
    ]
    for load in loads:
        load.start()
    loads[0].wait()

    lane_block = lax.broadcasted_iota(jnp.int32, (1, rows), 1) // BLK
    for slot, owner in enumerate(source + [me]):
        for b in range(nb):
            footw[slot, 0:1, b * BLK : (b + 1) * BLK] = foot[pl.ds(owner * nb + b, 1), :].astype(
                jnp.float32
            )
        columns = lane_block + owner * nb
        for b in range(nb):
            hit = jnp.zeros((1, rows), jnp.float32)
            for k in range(kb):
                hit = jnp.where(columns == blist[k, me * nb + b], 1.0, hit)
            act[0, slot, b : b + 1, :] = hit
        hits = [jnp.zeros((1, rows), jnp.float32) for _ in range(nb)]
        for k in range(kb):
            listed = jnp.full((1, rows), blist[k, owner * nb], jnp.int32)
            for b in range(1, nb):
                listed = jnp.where(lane_block == b, blist[k, owner * nb + b], listed)
            for b in range(nb):
                hits[b] = jnp.where(listed == me * nb + b, 1.0, hits[b])
        for b in range(nb):
            act[1, slot, b : b + 1, :] = hits[b]
    footc[...] = jnp.transpose(jnp.broadcast_to(footw[OWN, 0:1, :], (BLK, rows)))
    mx[...] = jnp.full(mx.shape, NEGATIVE, jnp.float32)
    sm[...] = jnp.zeros(sm.shape, jnp.float32)
    eye = lax.broadcasted_iota(jnp.int32, (BLK, BLK), 0) == lax.broadcasted_iota(
        jnp.int32, (BLK, BLK), 1
    )

    def stats(kind, slot, right, diag):
        for t in range(rows // tile):
            raw = lax.dot_general(
                own[kind, t * tile : (t + 1) * tile, :], right,
                (((1,), (1,)), ((), ())), preferred_element_type=jnp.float32,
            )
            for u in range(tile // BLK):
                b = t * (tile // BLK) + u
                span = slice(b * BLK, (b + 1) * BLK)
                top = mx[kind, span, :]
                new = top
                parts = []
                for j in range(nb):
                    cols = slice(j * BLK, (j + 1) * BLK)
                    valid = footc[span, :] != footw[slot, 0:1, cols]
                    if diag and j == b:
                        valid = jnp.logical_or(valid, eye)
                    valid = jnp.logical_and(valid, act[kind, slot, b : b + 1, cols] > 0.0)
                    part = jnp.where(valid, raw[u * BLK : (u + 1) * BLK, cols], NEGATIVE)
                    logit[kind, slot, span, cols] = part
                    parts.append(part)
                    new = jnp.maximum(new, part)
                total = sm[kind, span, :] * jnp.exp(top - new)
                for part in parts:
                    total = total + jnp.exp(part - new)
                mx[kind, span, :] = new
                sm[kind, span, :] = total

    def levels(kind):
        top = mx[kind]
        highest = jnp.max(top, axis=1, keepdims=True)
        total = jnp.sum(sm[kind] * jnp.exp(top - highest), axis=1, keepdims=True)
        wide = jnp.broadcast_to(highest + jnp.log(total), (rows, BLK))
        levc[kind] = wide
        levw[kind, OWN] = jnp.transpose(wide)[0:8, :]
        for role in range(ROLES):
            level_copy(kind, role).start()

    loads[1].wait()
    loads[2].wait()
    for kind in range(2):
        stats(kind, OWN, own[1 - kind], True)

    def landed(kind, slot):
        block = win.at[kind, slot]
        pltpu.make_async_copy(block, block, recv_sem.at[kind, slot]).wait()

    for kind in range(2):

        def near(slot, carry, kind=kind):
            landed(kind, slot)

            @pl.when(slot == 1)
            def _():
                hand_over(kind).start()

            @pl.when(slot == 1 + odd)
            def _():
                relay(kind).start()

            stats(kind, slot, win[kind, slot], False)
            return carry

        lax.fori_loop(0, 4, near, 0)

    for kind in range(2):

        def far(j, carry, kind=kind):
            slot = 4 + lax.rem(odd + j, 2)
            landed(kind, slot)

            @pl.when(j == 0)
            def _():
                share(kind).start()

            stats(kind, slot, win[kind, slot], False)
            return carry

        lax.fori_loop(0, 2, far, 0)
        levels(kind)

    def grads(kind, slot, right, out, diag):
        for t in range(rows // tile):
            pieces = []
            for u in range(tile // BLK):
                b = t * (tile // BLK) + u
                span = slice(b * BLK, (b + 1) * BLK)
                mine = levc[kind, span, :]
                across = []
                for j in range(nb):
                    cols = slice(j * BLK, (j + 1) * BLK)
                    part = logit[kind, slot, span, cols]
                    weight = 0.5 * (
                        jnp.exp(part - mine) + jnp.exp(part - levw[1 - kind, slot, 0:1, cols])
                    )
                    if diag and j == b:
                        weight = weight - jnp.where(eye, 1.0, 0.0)
                    across.append(weight.astype(jnp.bfloat16))
                pieces.append(jnp.concatenate(across, axis=1))
            weights = jnp.concatenate(pieces, axis=0)
            part = jnp.dot(weights, right, preferred_element_type=jnp.float32)
            span = slice(t * tile, (t + 1) * tile)
            if diag:
                out[span, :] = part
            else:
                out[span, :] = out[span, :] + part

    outs = (g1, g2)
    for kind in (1, 0):
        grads(kind, OWN, own[1 - kind], outs[kind], True)

        def step(role, carry, kind=kind):
            other = levw.at[1 - kind, role]
            pltpu.make_async_copy(other, other, lev_recv.at[1 - kind, role]).wait()
            grads(kind, role, win[kind, role], outs[kind], False)
            return carry

        lax.fori_loop(0, ROLES, step, 0)

    for kind in range(2):
        for role in range(3):
            direct(kind, role).wait_send()
        hand_over(kind).wait_send()
        relay(kind).wait_send()
        share(kind).wait_send()
        for role in range(ROLES):
            level_copy(kind, role).wait_send()


def shards(s1_embed, s2_embed, block_list, footprint):
    rows, width = s1_embed.shape
    n = lax.axis_size("row")
    foot = footprint.reshape(n * (rows // BLK), BLK)
    vmem = pl.BlockSpec(memory_space=pltpu.VMEM)
    hbm = pl.BlockSpec(memory_space=pltpu.HBM)
    return pl.pallas_call(
        functools.partial(kernel, n),
        out_shape=(
            jax.ShapeDtypeStruct((rows, width), jnp.float32),
            jax.ShapeDtypeStruct((rows, width), jnp.float32),
        ),
        in_specs=[hbm, hbm, pl.BlockSpec(memory_space=pltpu.SMEM), hbm],
        out_specs=(vmem, vmem),
        scratch_shapes=[
            pltpu.VMEM((2, rows, width), jnp.bfloat16),
            pltpu.VMEM(foot.shape, jnp.int32),
            pltpu.SemaphoreType.DMA((3,)),
            pltpu.VMEM((2, ROLES, rows, width), jnp.bfloat16),
            pltpu.VMEM((2, ROLES + 1, rows, rows), jnp.float32),
            pltpu.VMEM((2, ROLES + 1, 8, rows), jnp.float32),
            pltpu.VMEM((ROLES + 1, 8, rows), jnp.float32),
            pltpu.VMEM((rows, BLK), jnp.float32),
            pltpu.VMEM((2, rows, BLK), jnp.float32),
            pltpu.VMEM((2, rows, BLK), jnp.float32),
            pltpu.VMEM((2, rows, BLK), jnp.float32),
            pltpu.VMEM((2, ROLES + 1, 8, rows), jnp.float32),
            pltpu.SemaphoreType.DMA((2, ROLES)),
            pltpu.SemaphoreType.DMA((2, ROLES)),
            pltpu.SemaphoreType.DMA((2, ROLES)),
            pltpu.SemaphoreType.DMA((2, ROLES)),
        ],
        compiler_params=pltpu.CompilerParams(
            collective_id=0, has_side_effects=True, vmem_limit_bytes=63 * 1024 * 1024
        ),
    )(s1_embed, s2_embed, block_list.T, foot)


def solution(mesh):
    placed = (P(("grp", "row"), None), P(("grp", "row"), None), P("grp", None), P("grp"))
    return jax.shard_map(
        shards,
        mesh=mesh,
        in_specs=placed,
        out_specs=(P(("grp", "row"), None), P(("grp", "row"), None)),
        check_vma=False,
    )
```

```python
import functools

import jax
import jax.numpy as jnp
from jax import lax
from jax.experimental import pallas as pl
from jax.experimental.pallas import tpu as pltpu
from jax.sharding import PartitionSpec as P

BLK = 128
NEGATIVE = -1e30
ROLES = 6
PARTS = 4
OWN = 6
MESH = pl.DeviceIdType.MESH


def kernel(
    n, s1, s2, blist, foot_all, g1_out, g2_out,
    g1, g2, store_sem, own, foot, load_sem, win, logit, act, footw, footc, mx, sm, levc, levw,
    send_sem, recv_sem, lev_send, lev_recv,
):
    rows, width = s1.shape
    nb = rows // BLK
    kb = blist.shape[0]
    tile = min(256, rows)
    me = lax.axis_index("row")
    core = lax.rem(me, 2)
    chip = me // 2
    side = lax.rem(chip, 2)
    sgn = 1 - 2 * core
    sy = 1 - 2 * side
    odd = lax.rem(core + side, 2)

    def dev(offset):
        return lax.rem(me + offset + n, n)

    def at_chip(offset, which):
        return lax.rem(2 * (chip + offset) + which + n, n)

    partner, across, straight = dev(sgn), dev(2 * sy), dev(-3 * sgn)
    source = [
        partner, across, straight, dev(2 * sy + sgn), at_chip(-sy, 1 - side), at_chip(-sy, side)
    ]
    target = [partner, across, straight, dev(2 * sy + sgn), at_chip(-sy, 0), at_chip(-sy, 1)]
    landing = [0, 1, 2, 3, 4 + odd, 4 + odd]
    relay_to = dev(sy * (5 - 3 * odd))
    relay_peer = dev(sy * (5 - 10 * odd))

    barrier = pltpu.get_barrier_semaphore()
    for peer in target + [relay_peer]:
        pl.semaphore_signal(barrier, inc=1, device_id={"row": peer}, device_id_type=MESH)
    pl.semaphore_wait(barrier, ROLES + 1)

    own_right = (s2, s1)

    def direct(kind, role):
        return pltpu.make_async_remote_copy(
            src_ref=own_right[kind], dst_ref=win.at[kind, role],
            send_sem=send_sem.at[kind, role], recv_sem=recv_sem.at[kind, role],
            device_id={"row": target[role]}, device_id_type=MESH,
        )

    def passed(kind, held, slot, sem, to):
        return pltpu.make_async_remote_copy(
            src_ref=win.at[kind, held], dst_ref=win.at[kind, slot],
            send_sem=send_sem.at[kind, sem], recv_sem=recv_sem.at[kind, slot],
            device_id={"row": to}, device_id_type=MESH,
        )

    def hand_over(kind):
        return passed(kind, 1, 3, 3, partner)

    def relay(kind):
        return passed(kind, 1 + odd, 5 - odd, 4, relay_to)

    def share(kind):
        return passed(kind, 4 + odd, 4 + odd, 5, partner)

    def level_copy(kind, role):
        return pltpu.make_async_remote_copy(
            src_ref=levw.at[kind, OWN], dst_ref=levw.at[kind, landing[role]],
            send_sem=lev_send.at[kind, role], recv_sem=lev_recv.at[kind, landing[role]],
            device_id={"row": target[role]}, device_id_type=MESH,
        )

    for kind in range(2):
        for role in (2, 1, 0):
            direct(kind, role).start()

    loads = [
        pltpu.make_async_copy(foot_all, foot, load_sem.at[2]),
        pltpu.make_async_copy(s1, own.at[0], load_sem.at[0]),
        pltpu.make_async_copy(s2, own.at[1], load_sem.at[1]),
    ]
    for load in loads:
        load.start()
    loads[0].wait()

    lane_block = lax.broadcasted_iota(jnp.int32, (1, rows), 1) // BLK
    for slot, owner in enumerate(source + [me]):
        for b in range(nb):
            footw[slot, 0:1, b * BLK : (b + 1) * BLK] = foot[pl.ds(owner * nb + b, 1), :].astype(
                jnp.float32
            )
        columns = lane_block + owner * nb
        for b in range(nb):
            hit = jnp.zeros((1, rows), jnp.float32)
            for k in range(kb):
                hit = jnp.where(columns == blist[k, me * nb + b], 1.0, hit)
            act[0, slot, b : b + 1, :] = hit
        hits = [jnp.zeros((1, rows), jnp.float32) for _ in range(nb)]
        for k in range(kb):
            listed = jnp.full((1, rows), blist[k, owner * nb], jnp.int32)
            for b in range(1, nb):
                listed = jnp.where(lane_block == b, blist[k, owner * nb + b], listed)
            for b in range(nb):
                hits[b] = jnp.where(listed == me * nb + b, 1.0, hits[b])
        for b in range(nb):
            act[1, slot, b : b + 1, :] = hits[b]
    footc[...] = jnp.transpose(jnp.broadcast_to(footw[OWN, 0:1, :], (BLK, rows)))
    mx[...] = jnp.full(mx.shape, NEGATIVE, jnp.float32)
    sm[...] = jnp.zeros(sm.shape, jnp.float32)
    eye = lax.broadcasted_iota(jnp.int32, (BLK, BLK), 0) == lax.broadcasted_iota(
        jnp.int32, (BLK, BLK), 1
    )

    def stats(kind, slot, right, diag):
        for t in range(rows // tile):
            raw = lax.dot_general(
                own[kind, t * tile : (t + 1) * tile, :], right,
                (((1,), (1,)), ((), ())), preferred_element_type=jnp.float32,
            )
            for u in range(tile // BLK):
                b = t * (tile // BLK) + u
                span = slice(b * BLK, (b + 1) * BLK)
                top = mx[kind, span, :]
                new = top
                parts = []
                for j in range(nb):
                    cols = slice(j * BLK, (j + 1) * BLK)
                    valid = footc[span, :] != footw[slot, 0:1, cols]
                    if diag and j == b:
                        valid = jnp.logical_or(valid, eye)
                    valid = jnp.logical_and(valid, act[kind, slot, b : b + 1, cols] > 0.0)
                    part = jnp.where(valid, raw[u * BLK : (u + 1) * BLK, cols], NEGATIVE)
                    logit[kind, slot, span, cols] = part
                    parts.append(part)
                    new = jnp.maximum(new, part)
                total = sm[kind, span, :] * jnp.exp(top - new)
                for part in parts:
                    total = total + jnp.exp(part - new)
                mx[kind, span, :] = new
                sm[kind, span, :] = total

    def levels(kind):
        top = mx[kind]
        highest = jnp.max(top, axis=1, keepdims=True)
        total = jnp.sum(sm[kind] * jnp.exp(top - highest), axis=1, keepdims=True)
        wide = jnp.broadcast_to(highest + jnp.log(total), (rows, BLK))
        levc[kind] = wide
        levw[kind, OWN] = jnp.transpose(wide)[0:8, :]
        for role in range(ROLES):
            level_copy(kind, role).start()

    loads[1].wait()
    loads[2].wait()
    for kind in range(2):
        stats(kind, OWN, own[1 - kind], True)

    def landed(kind, slot):
        block = win.at[kind, slot]
        pltpu.make_async_copy(block, block, recv_sem.at[kind, slot]).wait()

    for kind in range(2):

        def near(slot, carry, kind=kind):
            landed(kind, slot)

            @pl.when(slot == 1)
            def _():
                hand_over(kind).start()

            @pl.when(slot == 1 + odd)
            def _():
                relay(kind).start()

            stats(kind, slot, win[kind, slot], False)
            return carry

        lax.fori_loop(0, 4, near, 0)

    for kind in range(2):

        def far(j, carry, kind=kind):
            slot = 4 + lax.rem(odd + j, 2)
            landed(kind, slot)

            @pl.when(j == 0)
            def _():
                share(kind).start()

            stats(kind, slot, win[kind, slot], False)
            return carry

        lax.fori_loop(0, 2, far, 0)
        levels(kind)

    def grads(kind, slot, right, out, diag):
        for t in range(rows // tile):
            pieces = []
            for u in range(tile // BLK):
                b = t * (tile // BLK) + u
                span = slice(b * BLK, (b + 1) * BLK)
                mine = levc[kind, span, :]
                across = []
                for j in range(nb):
                    cols = slice(j * BLK, (j + 1) * BLK)
                    part = logit[kind, slot, span, cols]
                    weight = 0.5 * (
                        jnp.exp(part - mine) + jnp.exp(part - levw[1 - kind, slot, 0:1, cols])
                    )
                    if diag and j == b:
                        weight = weight - jnp.where(eye, 1.0, 0.0)
                    across.append(weight.astype(jnp.bfloat16))
                pieces.append(jnp.concatenate(across, axis=1))
            weights = jnp.concatenate(pieces, axis=0)
            part = jnp.dot(weights, right, preferred_element_type=jnp.float32)
            span = slice(t * tile, (t + 1) * tile)
            if diag:
                out[span, :] = part
            else:
                out[span, :] = out[span, :] + part

    outs = (g1, g2)
    stores = [
        pltpu.make_async_copy(g1, g1_out, store_sem.at[0]),
        pltpu.make_async_copy(g2, g2_out, store_sem.at[1]),
    ]
    for kind in (1, 0):
        grads(kind, OWN, own[1 - kind], outs[kind], True)

        def step(role, carry, kind=kind):
            other = levw.at[1 - kind, role]
            pltpu.make_async_copy(other, other, lev_recv.at[1 - kind, role]).wait()
            grads(kind, role, win[kind, role], outs[kind], False)
            return carry

        lax.fori_loop(0, ROLES, step, 0)
        stores[kind].start()

    for kind in range(2):
        for role in range(3):
            direct(kind, role).wait_send()
        hand_over(kind).wait_send()
        relay(kind).wait_send()
        share(kind).wait_send()
        for role in range(ROLES):
            level_copy(kind, role).wait_send()
        stores[kind].wait()


def hand_out(a, b, a_out, b_out, held, in_sem, out_sem):
    size = a.shape[0] // PARTS

    def fetch(i, p):
        span = pl.ds(p * size, size)
        return pltpu.make_async_copy((a, b)[i].at[span, :], held.at[i, span, :], in_sem.at[i, p])

    def store(i, p):
        span = pl.ds(p * size, size)
        return pltpu.make_async_copy(
            held.at[i, span, :], (a_out, b_out)[i].at[span, :], out_sem.at[i, p]
        )

    order = [(i, p) for p in range(PARTS) for i in range(2)]
    for i, p in order:
        fetch(i, p).start()
    for i, p in order:
        fetch(i, p).wait()
        store(i, p).start()
    for i, p in order:
        store(i, p).wait()


def shards(s1_embed, s2_embed, block_list, footprint):
    rows, width = s1_embed.shape
    n = lax.axis_size("row")
    foot = footprint.reshape(n * (rows // BLK), BLK)
    hbm = pl.BlockSpec(memory_space=pltpu.HBM)
    made = pl.pallas_call(
        functools.partial(kernel, n),
        out_shape=(
            jax.ShapeDtypeStruct((rows, width), jnp.float32),
            jax.ShapeDtypeStruct((rows, width), jnp.float32),
        ),
        in_specs=[hbm, hbm, pl.BlockSpec(memory_space=pltpu.SMEM), hbm],
        out_specs=(hbm, hbm),
        scratch_shapes=[
            pltpu.VMEM((rows, width), jnp.float32),
            pltpu.VMEM((rows, width), jnp.float32),
            pltpu.SemaphoreType.DMA((2,)),
            pltpu.VMEM((2, rows, width), jnp.bfloat16),
            pltpu.VMEM(foot.shape, jnp.int32),
            pltpu.SemaphoreType.DMA((3,)),
            pltpu.VMEM((2, ROLES, rows, width), jnp.bfloat16),
            pltpu.VMEM((2, ROLES + 1, rows, rows), jnp.float32),
            pltpu.VMEM((2, ROLES + 1, 8, rows), jnp.float32),
            pltpu.VMEM((ROLES + 1, 8, rows), jnp.float32),
            pltpu.VMEM((rows, BLK), jnp.float32),
            pltpu.VMEM((2, rows, BLK), jnp.float32),
            pltpu.VMEM((2, rows, BLK), jnp.float32),
            pltpu.VMEM((2, rows, BLK), jnp.float32),
            pltpu.VMEM((2, ROLES + 1, 8, rows), jnp.float32),
            pltpu.SemaphoreType.DMA((2, ROLES)),
            pltpu.SemaphoreType.DMA((2, ROLES)),
            pltpu.SemaphoreType.DMA((2, ROLES)),
            pltpu.SemaphoreType.DMA((2, ROLES)),
        ],
        compiler_params=pltpu.CompilerParams(
            collective_id=0, has_side_effects=True, vmem_limit_bytes=63 * 1024 * 1024
        ),
    )(s1_embed, s2_embed, block_list.T, foot)
    return pl.pallas_call(
        hand_out,
        out_shape=(
            jax.ShapeDtypeStruct((rows, width), jnp.float32),
            jax.ShapeDtypeStruct((rows, width), jnp.float32),
        ),
        in_specs=[hbm, hbm],
        out_specs=(hbm, hbm),
        scratch_shapes=[
            pltpu.VMEM((2, rows, width), jnp.float32),
            pltpu.SemaphoreType.DMA((2, PARTS)),
            pltpu.SemaphoreType.DMA((2, PARTS)),
        ],
        compiler_params=pltpu.CompilerParams(vmem_limit_bytes=63 * 1024 * 1024),
    )(*made)


def solution(mesh):
    placed = (P(("grp", "row"), None), P(("grp", "row"), None), P("grp", None), P("grp"))
    return jax.shard_map(
        shards,
        mesh=mesh,
        in_specs=placed,
        out_specs=(P(("grp", "row"), None), P(("grp", "row"), None)),
        check_vma=False,
    )
```
